512 devices in a mesh: mem: 16 (over y, core), reg: 32 (over z, x).
Axes of the slice: x: 4, y: 8, z: 8, core: 2. Of those that a mesh axis runs over, the one named last changes fastest.
Arguments:
- perturb: float32 [256, 512, 1024], P('mem', 'reg'), may hold values from -6 to 6
- mean_state: float32 [512, 1024], P('reg'), may hold values from -6 to 6
- obs_pert: float32 [256, 256, 256], P('mem', 'reg'), may hold values from -6 to 6
- depart: float32 [256, 256], P('reg'), may hold values from -6 to 6
- inv_var: float32 [256, 256], P('reg'), may hold values from 0.01 to 0.1
- lists: int32 [512, 12], P('reg'), may hold values from 0 to 255, as said below
- counts: int32 [512], P('reg'), may hold values from 6 to 12
Outputs:
- analysis: float32 [256, 512, 1024], P('mem', 'reg')
The draws below stay inside these ranges and needn't reach their ends.
Inputs may be any that keep to these rules, and one draw needn't show every extreme that they name: `lists`: tile t lies in region t // 16; its list holds 12 different block ids, all from the blocks of regions t // 16 - 1, t // 16 and t // 16 + 1 (taken modulo the regions); block b belongs to region b // 8.
All inputs are finite; a program needn't handle non-finite values.
Results may differ from the reference program's by a relative error of at most 0.0003.
Values sent between devices are 32-bit elements; how exact they have to be, the bound alone decides.
A program may use at most 64 MiB of HBM per device.

```python
import math
import jax
import jax.numpy as jnp
from jax import lax

MEMBERS = 256
BLK_REG = 8
OBS_BLK = 256
NB = 12
ITERS = 6
TILE_GRP = 16
TILES = 512
CELLS = 1024
NBLK = 256


def draw_lists(key, part):
    key = jax.random.fold_in(key, 11)
    keys = jax.random.split(key, TILES)
    picks = jax.vmap(lambda single: jax.random.permutation(single, 3 * BLK_REG))(keys).astype(jnp.int32)
    first = picks[0]
    upper_end = BLK_REG - 1
    lower_end = BLK_REG
    swapped = jnp.where(first == upper_end, first[0], jnp.where(first == lower_end, first[1], first))
    swapped = swapped.at[0].set(upper_end).at[1].set(lower_end)
    picks = picks.at[0].set(swapped.astype(jnp.int32))
    picks = picks[:, :NB]
    region = jnp.arange(TILES, dtype=jnp.int32) // TILE_GRP
    ids = jnp.mod((region[:, None] - 1) * BLK_REG + picks, NBLK)
    return ids.astype(jnp.int32)


def draw_counts(key, part):
    key = jax.random.fold_in(key, 23)
    lowest = (NB + 1) // 2
    values = jax.random.randint(key, (TILES,), lowest, NB + 1, dtype=jnp.int32)
    values = values.at[0].set(NB)
    values = values.at[TILES - 1].set(lowest)
    return values.astype(jnp.int32)


def level_of(rng, shape, cuts, low, high):
    loudness = 1.0
    for position, shards_of in cuts:
        steps = jax.random.uniform(jax.random.fold_in(jax.random.fold_in(rng, 6), position), (shards_of,), jnp.float32, low / len(cuts), high / len(cuts))
        loudness = loudness * jnp.repeat(jnp.exp(steps), shape[position] // shards_of).reshape((-1,) + (1,) * (len(shape) - 1 - position))
    return loudness


def centred(rng, shape, width, reach, pieces=(), kind=jnp.bfloat16):
    values = width * jax.random.normal(rng, shape, jnp.float32)
    if pieces:
        values = values * level_of(rng, shape, pieces, -0.22, 0.18)
    return jnp.clip(values, -reach, reach).astype(kind)


def setup_inputs(seed: int = 0) -> dict:
    key_of = jax.random.split(jax.random.key(seed), 8)
    perturb = centred(key_of[0], (MEMBERS, TILES, CELLS), 1.0, 6.0, ((0, 16), (1, 32)), jnp.float32)
    mean_state = centred(key_of[1], (TILES, CELLS), 1.0, 6.0, ((0, 32),), jnp.float32)
    obs_pert = centred(key_of[2], (MEMBERS, NBLK, OBS_BLK), 1.0, 6.0, ((0, 16), (1, 32)), jnp.float32)
    depart = centred(key_of[3], (NBLK, OBS_BLK), 1.0, 6.0, ((0, 32),), jnp.float32)
    inv_var = jnp.clip(jnp.exp(math.log(0.1) - 2.3025851 * jax.random.uniform(key_of[4], (NBLK, OBS_BLK), jnp.float32) ** level_of(key_of[4], (NBLK, OBS_BLK), ((0, 32),), -0.2, 0.2)), 0.01, 0.1)
    lists = draw_lists(jax.random.fold_in(key_of[7], 71), 0)
    counts = draw_counts(jax.random.fold_in(key_of[7], 71), 0)
    return dict(perturb=perturb, mean_state=mean_state, obs_pert=obs_pert, depart=depart, inv_var=inv_var, lists=lists, counts=counts)


def tile_terms(ensemble, departures, variances, block_ids, live_count):
    members = ensemble.shape[0]
    chosen = jnp.take(ensemble, block_ids, axis=1).reshape(members, -1)
    live = (jnp.arange(block_ids.shape[0]) < live_count).astype(jnp.float32)
    weights = (jnp.take(variances, block_ids, axis=0) * live[:, None]).reshape(-1)
    values = jnp.take(departures, block_ids, axis=0).reshape(-1)
    weighted = chosen * weights[None, :]
    square = jnp.dot(weighted, chosen.T, precision=lax.Precision.HIGHEST, preferred_element_type=jnp.float32)
    vector = jnp.dot(weighted, values, precision=lax.Precision.HIGHEST, preferred_element_type=jnp.float32)
    return jnp.concatenate([square, vector[None, :]], axis=0)

def analysis_weights(term):
    members = term.shape[1]
    square = term[:members]
    vector = term[members]
    eye = jnp.eye(members, dtype=jnp.float32)
    precision_matrix = square + (members - 1.0) * eye
    scale_total = jnp.trace(precision_matrix) - (members - 1.0) * (members - 1.0)
    iterate = precision_matrix / scale_total
    inverse_root = eye
    for step in range(ITERS):
        middle = 1.5 * eye - 0.5 * jnp.dot(inverse_root, iterate, precision=lax.Precision.HIGHEST)
        iterate = jnp.dot(iterate, middle, precision=lax.Precision.HIGHEST)
        inverse_root = jnp.dot(middle, inverse_root, precision=lax.Precision.HIGHEST)
    spread_weights = jnp.sqrt((members - 1.0) / scale_total) * inverse_root
    inner = jnp.dot(inverse_root, vector, precision=lax.Precision.HIGHEST)
    mean_weights = jnp.dot(inverse_root, inner, precision=lax.Precision.HIGHEST) / scale_total
    return spread_weights + mean_weights[:, None]

def reference(perturb, mean_state, obs_pert, depart, inv_var, lists, counts):

    def one_tile(tile):
        term = tile_terms(obs_pert, depart, inv_var, lists[tile], counts[tile])
        combined = analysis_weights(term)
        background = perturb[:, tile, :]
        moved = jnp.dot(combined.T, background, precision=lax.Precision.HIGHEST, preferred_element_type=jnp.float32)
        return mean_state[tile][None, :] + moved
    result = lax.map(one_tile, jnp.arange(TILES, dtype=jnp.int32))
    return jnp.transpose(result, (1, 0, 2))
```

```python
import functools

import jax
import jax.numpy as jnp
from jax import lax
from jax.experimental import pallas as pl
from jax.experimental.pallas import tpu as pltpu
from jax.sharding import PartitionSpec as P

ITERS = 6
PLAN = ((), (1, 7, 0), (4,), (2, 6), (3, 5))

MESH = pl.DeviceIdType.MESH
NT = (((1,), (1,)), ((), ()))
NN = (((1,), (0,)), ((), ()))


def split(a):
    hi = a.astype(jnp.bfloat16)
    return hi, (a - hi.astype(jnp.float32)).astype(jnp.bfloat16)


def dot3(a, b, dims=NN):
    def one(x, y):
        return lax.dot_general(x, y, dims, preferred_element_type=jnp.float32)

    return one(a[0], b[0]) + (one(a[0], b[1]) + one(a[1], b[0]))


def kernel(
    n,
    regions,
    counts_in,
    lists_in,
    obs_in,
    depart_in,
    inv_in,
    mean_in,
    perturb_ref,
    out_ref,
    counts_ref,
    lists_ref,
    obs_ref,
    depart_ref,
    inv_ref,
    mean_ref,
    xa,
    cp,
    pr,
    cf,
    cs,
    ex,
    sp,
    sr,
    xin,
    og,
    hi_ref,
    lo_ref,
    send_sem,
    recv_sem,
    near_send,
    near_recv,
    pair_send,
    pair_recv,
    local_sem,
    group_in,
    near_in,
):
    me = lax.axis_index("mem")
    region = lax.axis_index("reg")
    right = lax.rem(region + 1, regions)
    left = lax.rem(region + regions - 1, regions)
    blocks = depart_in.shape[0]
    group = obs_in.shape[0]
    members = n * group
    half = members // 2
    others = n - 1
    chips = n // 2
    chip = me // 2
    core = lax.rem(me, 2)

    def partner(j):
        return 2 * lax.rem(chip + j // 2, chips) + lax.rem(core + lax.rem(j, 2), 2)

    def place(i):
        pair = i // 2
        ahead = chips // 2 + ((pair + 1) // 2) * (1 - 2 * lax.rem(pair, 2))
        return 2 * ahead + 1 - lax.rem(i, 2)

    def exchange(phase, source, target):
        def copy(j):
            to = partner(j)
            return pltpu.make_async_remote_copy(
                src_ref=source(to),
                dst_ref=target(me),
                send_sem=send_sem.at[phase, j],
                recv_sem=recv_sem.at[phase, j],
                device_id=(to, region),
                device_id_type=MESH,
            )

        return copy

    def each(action):
        def body(i, carry):
            action(place(i))
            return carry

        lax.fori_loop(0, others, body, 0)

    def each_now(action):
        for i in range(others):
            pair = i // 2
            ahead = chips // 2 + ((pair + 1) // 2) * (1 - 2 * (pair % 2))
            action(2 * ahead + 1 - i % 2)

    def near(slot, source, low, high):
        first = pltpu.make_async_remote_copy(
            src_ref=source,
            dst_ref=low,
            send_sem=near_send.at[slot],
            recv_sem=near_recv.at[slot],
            device_id=(me, right),
            device_id_type=MESH,
        )
        second = pltpu.make_async_remote_copy(
            src_ref=source,
            dst_ref=high,
            send_sem=near_send.at[slot + 1],
            recv_sem=near_recv.at[slot + 1],
            device_id=(me, left),
            device_id_type=MESH,
        )
        return first, second

    leads = me == 0
    follows = me != 0
    barrier = pltpu.get_barrier_semaphore()

    def greet(j):
        to = partner(j)

        @pl.when(to != 0)
        def _():
            pl.semaphore_signal(
                barrier, inc=1, device_id=(to, region), device_id_type=MESH
            )

    each(greet)

    loads = [
        pltpu.make_async_copy(source, target, local_sem.at[3 + at])
        for at, (source, target) in enumerate(
            (
                (counts_in, counts_ref),
                (lists_in, lists_ref),
                (obs_in, obs_ref),
                (depart_in, depart_ref),
                (inv_in, inv_ref),
                (mean_in.at[pl.ds(me, 1)], mean_ref),
            )
        )
    ]
    for load in loads:
        load.start()
    own_background = pltpu.make_async_copy(
        perturb_ref.at[:, me, :], xin.at[me], local_sem.at[1]
    )
    own_background.start()
    background = exchange(
        3, lambda to: perturb_ref.at[:, to, :], lambda slot: xin.at[slot]
    )

    @pl.when(follows)
    def _():
        pl.semaphore_wait(barrier, others)

    @pl.when(me == 1)
    def _():
        pl.semaphore_signal(
            group_in, inc=1, device_id=(0, region), device_id_type=MESH
        )
        for side in (left, right):
            pl.semaphore_signal(
                barrier, inc=1, device_id=(0, side), device_id_type=MESH
            )

    @pl.when(leads)
    def _():
        pl.semaphore_wait(group_in, 1)

    def piece(to):
        return obs_in.at[
            :, to // 2, pl.ds(pl.multiple_of(lax.rem(to, 2) * 128, 128), 128)
        ]

    obs_copy = exchange(0, piece, lambda slot: xa.at[slot])

    def send_background(point):
        for ahead in PLAN[point]:
            for flip in (0, 1):
                if ahead or flip:
                    background(2 * ahead + flip).start()

    send_background(0)
    each_now(lambda j: obs_copy(j).start())
    own_obs = pltpu.make_async_copy(piece(me), xa.at[me], local_sem.at[0])
    own_obs.start()
    send_background(1)
    for load in loads:
        load.wait()

    tile_row = lax.broadcasted_iota(jnp.int32, (n, 128), 0)
    lane = lax.broadcasted_iota(jnp.int32, (n, 128), 1)
    live = jnp.zeros((n, 128), jnp.int32)
    for t in range(n):
        live = jnp.where(tile_row == t, counts_ref[t], live)
    total = blocks * regions
    local = lax.rem(lists_ref[...] - region * blocks + (blocks + total), total)
    chosen = jnp.zeros((n, 128), jnp.float32)
    for j in range(lists_ref.shape[1]):
        hit = (lane == local[:, j : j + 1]) & (live > j)
        chosen = jnp.where(hit, 1.0, chosen)
    chosen = chosen[:, : 3 * blocks].astype(jnp.bfloat16)

    weights = inv_ref[...]
    weighted_departures = weights * depart_ref[...]
    extra_lane = lax.broadcasted_iota(jnp.int32, (blocks, 128), 1)
    extras = jnp.zeros((blocks, 128), jnp.float32)
    for i in range(group):
        one = obs_ref[i]
        vector = jnp.sum(one * weighted_departures, axis=1, keepdims=True)
        diagonal = jnp.sum(one * one * weights, axis=1, keepdims=True)
        extras = jnp.where(extra_lane == i, vector, extras)
        extras = jnp.where(extra_lane == group + i, diagonal, extras)
    ex[1] = extras

    def combine(values):
        top = values.astype(jnp.bfloat16)
        rest = values - top.astype(jnp.float32)
        middle = rest.astype(jnp.bfloat16)
        last = (rest - middle.astype(jnp.float32)).astype(jnp.bfloat16)
        parts = [
            jnp.dot(chosen, part, preferred_element_type=jnp.float32)
            for part in (top, middle, last)
        ]
        return parts[0] + (parts[1] + parts[2])

    own_obs.wait()
    each(lambda j: obs_copy(j).wait_recv())
    x = xa[...].reshape(members, 128)
    block_row = lax.broadcasted_iota(jnp.int32, weights.shape, 0)
    w = jnp.sum(
        jnp.where(block_row == me // 2, weights, 0.0), axis=0, keepdims=True
    )
    w = jnp.where(lax.rem(me, 2) == 0, w[:, :128], w[:, 128:])
    square = dot3(split(x * w), split(x), NT)
    row = lax.broadcasted_iota(jnp.int32, (half, half), 0)
    column = lax.broadcasted_iota(jnp.int32, (half, half), 1)
    cp[0] = square[:half, half:].reshape(n, group // 2, 128)
    cp[1] = jnp.where(
        row >= column, square[:half, :half], square[half:, half:]
    ).reshape(n, group // 2, 128)
    pair_copy = pltpu.make_async_remote_copy(
        src_ref=cp.at[1 - core],
        dst_ref=pr,
        send_sem=pair_send,
        recv_sem=pair_recv,
        device_id=(2 * chip + 1 - core, region),
        device_id_type=MESH,
    )
    pair_copy.start()
    pair_copy.wait_recv()
    cf[...] = cp[core] + pr[...]
    square_copy = exchange(
        1, lambda to: cf.at[to], lambda slot: cs.at[1, slot // 2, lax.rem(slot, 2)]
    )
    each_now(lambda j: square_copy(j).start())
    send_background(2)
    cs[1, chip, core] = cf[me]

    def pass_word(j):
        pl.semaphore_signal(
            near_in, inc=1, device_id=(partner(j), region), device_id_type=MESH
        )

    @pl.when(leads)
    def _():
        pl.semaphore_wait(barrier, 2)
        each_now(pass_word)

    @pl.when(follows)
    def _():
        pl.semaphore_wait(near_in, 1)

    extra_near = near(0, ex.at[1], ex.at[0], ex.at[2])
    for copy in extra_near:
        copy.start()

    def near_square(b, at):
        return near(
            2 + 2 * at, cs.at[1, b], cs.at[0, b], cs.at[2, b]
        )

    def pass_on(at, carry):
        ahead = chips // 2 + ((at + 1) // 2) * (1 - 2 * lax.rem(at, 2))

        @pl.when(ahead != 0)
        def _():
            square_copy(2 * ahead).wait_recv()

        square_copy(2 * ahead + 1).wait_recv()
        for copy in near_square(lax.rem(chip - ahead + chips, chips), at):
            copy.start()
        return carry

    lax.fori_loop(0, chips, pass_on, 0)
    send_background(3)

    def take_near(at, carry):
        for copy in near_square(at, at):
            copy.wait_recv()
        return carry

    lax.fori_loop(0, chips, take_near, 0)
    for copy in extra_near:
        copy.wait_recv()
    sp[:, group, :] = combine(ex[...].reshape(3 * blocks, 128))
    near_squares = jnp.concatenate(
        [
            cs[:, :, i // 8, i % 8, :].reshape(3 * blocks, 128)
            for i in range(group)
        ],
        axis=1,
    )
    tile_squares = combine(near_squares)
    for i in range(group):
        sp[:, i, :] = tile_squares[:, i * 128 : (i + 1) * 128]
    used = pl.ds(0, group + 1)
    tile_copy = exchange(
        2, lambda to: sp.at[to, used], lambda slot: sr.at[slot, used]
    )
    each_now(lambda j: tile_copy(j).start())
    sr[pl.ds(me, 1)] = sp[pl.ds(me, 1)]
    send_background(4)

    each(lambda j: tile_copy(j).wait_recv())
    got = sr[:, group, :]
    got_lane = lax.broadcasted_iota(jnp.int32, got.shape, 1)

    def spread_out(values):
        kept = jnp.where(got_lane < group, values, 0.0)
        per_row = 128 // group
        return jnp.concatenate(
            [
                jnp.sum(
                    pltpu.roll(
                        kept[at : at + per_row], 0, 1, stride=group, stride_axis=0
                    ),
                    axis=0,
                    keepdims=True,
                )
                for at in range(0, n, per_row)
            ],
            axis=1,
        )

    vector = spread_out(got)
    diagonal = spread_out(pltpu.roll(got, 128 - group, 1))
    scale_total = jnp.sum(diagonal, axis=1, keepdims=True) + (members - 1.0)
    inverse_scale = 1.0 / scale_total

    corner = sr[:, : group // 2].reshape(half, 128)
    both = sr[:, group // 2 : group].reshape(half, 128)
    flipped = both.T
    lower = jnp.where(row > column, both, flipped)
    upper = jnp.where(row < column, both, flipped)
    full = jnp.concatenate(
        [
            jnp.concatenate([lower, corner], axis=1),
            jnp.concatenate([corner.T, upper], axis=1),
        ],
        axis=0,
    )
    full_row = lax.broadcasted_iota(jnp.int32, (members, members), 0)
    full_column = lax.broadcasted_iota(jnp.int32, (members, members), 1)
    on_diagonal = full_row == full_column
    full = jnp.where(on_diagonal, diagonal + (members - 1.0), full) * inverse_scale

    def middle_of(product):
        return jnp.where(on_diagonal, 1.5, 0.0) - 0.5 * product

    def store(where, values):
        hi, lo = split(values)
        hi_ref[where] = hi
        lo_ref[where] = lo

    top, bottom = pl.ds(0, members), pl.ds(members, members)

    def product():
        return dot3(
            (hi_ref[bottom], lo_ref[bottom]), (hi_ref[top], lo_ref[top])
        )

    first = middle_of(full)
    store(top, dot3(split(full), split(first)))
    store(bottom, first)

    def iterate(step, carry):
        middle = split(middle_of(product()))
        store(pl.ds(0, 2 * members), dot3((hi_ref[...], lo_ref[...]), middle))
        return carry

    lax.fori_loop(1, ITERS - 1, iterate, 0)
    middle = split(middle_of(product()))
    inverse_root = dot3((hi_ref[bottom], lo_ref[bottom]), middle)
    root_parts = split(inverse_root)
    inner = dot3(split(jnp.broadcast_to(vector, (8, members))), root_parts)
    shift = dot3(split(inner), root_parts)[0:1] * inverse_scale
    spread = jnp.sqrt((members - 1.0) * inverse_scale)
    combined = split(inverse_root * spread + shift)

    own_background.wait()
    each(lambda j: background(j).wait_recv())
    values = split(xin[...].reshape(members, xin.shape[2]))
    mean = mean_ref[...]
    og[...] = (dot3(combined, values) + mean).reshape(og.shape)
    result_copy = exchange(
        4, lambda to: og.at[to], lambda slot: out_ref.at[:, slot, :]
    )
    each_now(lambda j: result_copy(j).start())
    own_result = pltpu.make_async_copy(
        og.at[me], out_ref.at[:, me, :], local_sem.at[2]
    )
    own_result.start()
    own_result.wait()
    for copy in extra_near:
        copy.wait_send()
    pair_copy.wait_send()

    def near_sent(at, carry):
        for copy in near_square(at, at):
            copy.wait_send()
        return carry

    lax.fori_loop(0, chips, near_sent, 0)
    for copies in (obs_copy, square_copy, tile_copy, background):
        each(lambda j: copies(j).wait_send())
    each(lambda j: result_copy(j).wait())


def on_device(n, regions, perturb, mean_state, obs_pert, depart, inv_var, lists, counts):
    group, tiles, cells = perturb.shape
    blocks = depart.shape[0]
    members = n * group
    f32 = jnp.float32
    hbm = pl.BlockSpec(memory_space=pltpu.HBM)
    return pl.pallas_call(
        functools.partial(kernel, n, regions),
        out_shape=jax.ShapeDtypeStruct((group, tiles, cells), f32),
        in_specs=[hbm] * 7,
        out_specs=pl.BlockSpec(memory_space=pl.ANY),
        scratch_shapes=[
            pltpu.SMEM(counts.shape, jnp.int32),
            pltpu.VMEM(lists.shape, jnp.int32),
            pltpu.VMEM(obs_pert.shape, f32),
            pltpu.VMEM(depart.shape, f32),
            pltpu.VMEM(inv_var.shape, f32),
            pltpu.VMEM((1, cells), f32),
            pltpu.VMEM((n, group, 128), f32),
            pltpu.VMEM((2, n, group // 2, 128), f32),
            pltpu.VMEM((n, group // 2, 128), f32),
            pltpu.VMEM((n, group // 2, 128), f32),
            pltpu.VMEM((3, blocks, 2, group // 2, 128), f32),
            pltpu.VMEM((3, blocks, 128), f32),
            pltpu.VMEM((n, group + 8, 128), f32),
            pltpu.VMEM((n, group + 8, 128), f32),
            pltpu.VMEM((n, group, cells), f32),
            pltpu.VMEM((n, group, cells), f32),
            pltpu.VMEM((2 * members, members), jnp.bfloat16),
            pltpu.VMEM((2 * members, members), jnp.bfloat16),
            pltpu.SemaphoreType.DMA((5, n)),
            pltpu.SemaphoreType.DMA((5, n)),
            pltpu.SemaphoreType.DMA((2 + 2 * blocks,)),
            pltpu.SemaphoreType.DMA((2 + 2 * blocks,)),
            pltpu.SemaphoreType.DMA,
            pltpu.SemaphoreType.DMA,
            pltpu.SemaphoreType.DMA((9,)),
            pltpu.SemaphoreType.REGULAR,
            pltpu.SemaphoreType.REGULAR,
        ],
        compiler_params=pltpu.CompilerParams(
            collective_id=0, has_side_effects=True, vmem_limit_bytes=32 * 2**20
        ),
        name="analysis",
    )(
        *[
            pltpu.with_memory_space_constraint(value, pltpu.HBM)
            for value in (counts, lists, obs_pert, depart, inv_var, mean_state, perturb)
        ]
    )


def solution(mesh):
    placed = (
        P("mem", "reg", None),
        P("reg", None),
        P("mem", "reg", None),
        P("reg", None),
        P("reg", None),
        P("reg", None),
        P("reg"),
    )
    return jax.shard_map(
        functools.partial(on_device, mesh.shape["mem"], mesh.shape["reg"]),
        mesh=mesh,
        in_specs=placed,
        out_specs=P("mem", "reg", None),
        check_vma=False,
    )
```

```python
import functools

import jax
import jax.numpy as jnp
from jax import lax
from jax.experimental import pallas as pl
from jax.experimental.pallas import tpu as pltpu
from jax.sharding import PartitionSpec as P

ITERS = 6
PLAN = ((), (4,), (2, 6), (1, 7, 0), (3, 5))
FIRST = ((), (3, 5), (4,), (1, 7, 0), (2, 6))
LAST = ((), (4,), (), (1, 7, 0, 2, 6), (3, 5))

MESH = pl.DeviceIdType.MESH
NT = (((1,), (1,)), ((), ()))
NN = (((1,), (0,)), ((), ()))


def split(a):
    hi = a.astype(jnp.bfloat16)
    return hi, (a - hi.astype(jnp.float32)).astype(jnp.bfloat16)


def dot3(a, b, dims=NN):
    def one(x, y):
        return lax.dot_general(x, y, dims, preferred_element_type=jnp.float32)

    return one(a[0], b[0]) + (one(a[0], b[1]) + one(a[1], b[0]))


def kernel(
    n,
    regions,
    counts_in,
    lists_in,
    obs_in,
    depart_in,
    inv_in,
    mean_in,
    perturb_ref,
    out_ref,
    counts_ref,
    lists_ref,
    obs_ref,
    depart_ref,
    inv_ref,
    mean_ref,
    xa,
    cp,
    pr,
    cf,
    cs,
    ex,
    sp,
    sr,
    xin,
    og,
    hi_ref,
    lo_ref,
    send_sem,
    recv_sem,
    chip_sem,
    near_send,
    near_recv,
    pair_send,
    pair_recv,
    local_sem,
    group_in,
    near_in,
):
    me = lax.axis_index("mem")
    region = lax.axis_index("reg")
    right = lax.rem(region + 1, regions)
    left = lax.rem(region + regions - 1, regions)
    blocks = depart_in.shape[0]
    group = obs_in.shape[0]
    members = n * group
    half = members // 2
    others = n - 1
    chips = n // 2
    chip = me // 2
    core = lax.rem(me, 2)

    def partner(j):
        return 2 * lax.rem(chip + j // 2, chips) + lax.rem(core + lax.rem(j, 2), 2)

    def exchange(phase, source, target, arrival=None):
        def copy(j):
            to = partner(j)
            landed = recv_sem.at[phase] if arrival is None else arrival(j)
            return pltpu.make_async_remote_copy(
                src_ref=source(to),
                dst_ref=target(me),
                send_sem=send_sem.at[phase],
                recv_sem=landed,
                device_id=(to, region),
                device_id_type=MESH,
            )

        return copy

    def take(ref, sem):
        pltpu.make_async_copy(ref, ref, sem).wait()

    all_but_one = pl.ds(0, others)

    chip_order = [
        chips // 2 + (i + 1) // 2 * (1 - 2 * (i % 2)) for i in range(chips)
    ]

    def each(action):
        for ahead in chip_order:
            for flip in (1, 0):
                if ahead or flip:
                    action(2 * ahead + flip)

    def near(slot, source, low, high):
        first = pltpu.make_async_remote_copy(
            src_ref=source,
            dst_ref=low,
            send_sem=near_send.at[slot],
            recv_sem=near_recv.at[slot],
            device_id=(me, right),
            device_id_type=MESH,
        )
        second = pltpu.make_async_remote_copy(
            src_ref=source,
            dst_ref=high,
            send_sem=near_send.at[slot + 1],
            recv_sem=near_recv.at[slot + 1],
            device_id=(me, left),
            device_id_type=MESH,
        )
        return first, second

    leads = me == 0
    follows = me != 0
    barrier = pltpu.get_barrier_semaphore()

    def greet(j):
        to = partner(j)

        @pl.when(to != 0)
        def _():
            pl.semaphore_signal(
                barrier, inc=1, device_id=(to, region), device_id_type=MESH
            )

    each(greet)

    loads = [
        pltpu.make_async_copy(source, target, local_sem.at[3 + at])
        for at, (source, target) in enumerate(
            (
                (counts_in, counts_ref),
                (lists_in, lists_ref),
                (obs_in, obs_ref),
                (depart_in, depart_ref),
                (inv_in, inv_ref),
                (mean_in.at[pl.ds(me, 1)], mean_ref),
            )
        )
    ]
    for load in loads:
        load.start()
    own_background = pltpu.make_async_copy(
        perturb_ref.at[:, me, :], xin.at[me], local_sem.at[1]
    )
    own_background.start()
    background = exchange(
        3, lambda to: perturb_ref.at[:, to, :], lambda slot: xin.at[slot]
    )

    @pl.when(follows)
    def _():
        pl.semaphore_wait(barrier, others)

    @pl.when(me == 1)
    def _():
        pl.semaphore_signal(
            group_in, inc=1, device_id=(0, region), device_id_type=MESH
        )
        for side in (left, right):
            pl.semaphore_signal(
                barrier, inc=1, device_id=(0, side), device_id_type=MESH
            )

    @pl.when(leads)
    def _():
        pl.semaphore_wait(group_in, 1)

    def piece(to):
        return obs_in.at[
            :, to // 2, pl.ds(pl.multiple_of(lax.rem(to, 2) * 128, 128), 128)
        ]

    obs_copy = exchange(0, piece, lambda slot: xa.at[slot])

    def send_background(point):
        begins, ends = region == 0, region == regions - 1
        for here, plan in (
            (begins, FIRST),
            (ends, LAST),
            (jnp.logical_not(begins | ends), PLAN),
        ):
            if not plan[point]:
                continue

            @pl.when(here)
            def _(plan=plan):
                for ahead in plan[point]:
                    for flip in (0, 1):
                        if ahead or flip:
                            background(2 * ahead + flip).start()

    send_background(0)
    each(lambda j: obs_copy(j).start())
    own_obs = pltpu.make_async_copy(piece(me), xa.at[me], local_sem.at[0])
    own_obs.start()
    send_background(1)
    for load in loads:
        load.wait()

    tile_row = lax.broadcasted_iota(jnp.int32, (n, 128), 0)
    lane = lax.broadcasted_iota(jnp.int32, (n, 128), 1)
    live = jnp.zeros((n, 128), jnp.int32)
    for t in range(n):
        live = jnp.where(tile_row == t, counts_ref[t], live)
    total = blocks * regions
    local = lax.rem(lists_ref[...] - region * blocks + (blocks + total), total)
    chosen = jnp.zeros((n, 128), jnp.float32)
    for j in range(lists_ref.shape[1]):
        hit = (lane == local[:, j : j + 1]) & (live > j)
        chosen = jnp.where(hit, 1.0, chosen)
    chosen = chosen[:, : 3 * blocks].astype(jnp.bfloat16)

    weights = inv_ref[...]
    weighted_departures = weights * depart_ref[...]
    extra_lane = lax.broadcasted_iota(jnp.int32, (blocks, 128), 1)
    extras = jnp.zeros((blocks, 128), jnp.float32)
    for i in range(group):
        one = obs_ref[i]
        vector = jnp.sum(one * weighted_departures, axis=1, keepdims=True)
        diagonal = jnp.sum(one * one * weights, axis=1, keepdims=True)
        extras = jnp.where(extra_lane == i, vector, extras)
        extras = jnp.where(extra_lane == group + i, diagonal, extras)
    ex[1] = extras

    def combine(values):
        top = values.astype(jnp.bfloat16)
        rest = values - top.astype(jnp.float32)
        middle = rest.astype(jnp.bfloat16)
        last = (rest - middle.astype(jnp.float32)).astype(jnp.bfloat16)
        parts = [
            jnp.dot(chosen, part, preferred_element_type=jnp.float32)
            for part in (top, middle, last)
        ]
        return parts[0] + (parts[1] + parts[2])

    own_obs.wait()
    take(xa.at[all_but_one], recv_sem.at[0])
    x = xa[...].reshape(members, 128)
    block_row = lax.broadcasted_iota(jnp.int32, weights.shape, 0)
    w = jnp.sum(
        jnp.where(block_row == me // 2, weights, 0.0), axis=0, keepdims=True
    )
    w = jnp.where(lax.rem(me, 2) == 0, w[:, :128], w[:, 128:])
    square = dot3(split(x * w), split(x), NT)
    row = lax.broadcasted_iota(jnp.int32, (half, half), 0)
    column = lax.broadcasted_iota(jnp.int32, (half, half), 1)
    cp[0] = square[:half, half:].reshape(n, group // 2, 128)
    cp[1] = jnp.where(
        row >= column, square[:half, :half], square[half:, half:]
    ).reshape(n, group // 2, 128)
    pair_copy = pltpu.make_async_remote_copy(
        src_ref=cp.at[1 - core],
        dst_ref=pr,
        send_sem=pair_send,
        recv_sem=pair_recv,
        device_id=(2 * chip + 1 - core, region),
        device_id_type=MESH,
    )
    pair_copy.start()
    pair_copy.wait_recv()
    cf[...] = cp[core] + pr[...]
    square_copy = exchange(
        1,
        lambda to: cf.at[to],
        lambda slot: cs.at[1, slot // 2, lax.rem(slot, 2)],
        lambda j: chip_sem.at[j // 2],
    )
    each(lambda j: square_copy(j).start())
    send_background(2)
    cs[1, chip, core] = cf[me]

    def pass_word(j):
        pl.semaphore_signal(
            near_in, inc=1, device_id=(partner(j), region), device_id_type=MESH
        )

    @pl.when(leads)
    def _():
        pl.semaphore_wait(barrier, 2)
        each(pass_word)

    @pl.when(follows)
    def _():
        pl.semaphore_wait(near_in, 1)

    extra_near = near(0, ex.at[1], ex.at[0], ex.at[2])
    for copy in extra_near:
        copy.start()

    for ahead in chip_order:
        take(cs.at[1, 0] if ahead else cs.at[1, 0, 0], chip_sem.at[ahead])
        b = lax.rem(chip - ahead + chips, chips)
        for copy in near(2, cs.at[1, b], cs.at[0, b], cs.at[2, b]):
            copy.start()
    send_background(3)

    take(cs.at[0], near_recv.at[2])
    take(cs.at[2], near_recv.at[3])
    for copy in extra_near:
        copy.wait_recv()
    sp[:, group, :] = combine(ex[...].reshape(3 * blocks, 128))
    near_squares = jnp.concatenate(
        [
            cs[:, :, i // 8, i % 8, :].reshape(3 * blocks, 128)
            for i in range(group)
        ],
        axis=1,
    )
    tile_squares = combine(near_squares)
    for i in range(group):
        sp[:, i, :] = tile_squares[:, i * 128 : (i + 1) * 128]
    used = pl.ds(0, group + 1)
    tile_copy = exchange(
        2, lambda to: sp.at[to, used], lambda slot: sr.at[slot, used]
    )
    each(lambda j: tile_copy(j).start())
    sr[pl.ds(me, 1)] = sp[pl.ds(me, 1)]
    send_background(4)

    take(sr.at[all_but_one, used], recv_sem.at[2])
    got = sr[:, group, :]
    got_lane = lax.broadcasted_iota(jnp.int32, got.shape, 1)

    def spread_out(values):
        kept = jnp.where(got_lane < group, values, 0.0)
        per_row = 128 // group
        return jnp.concatenate(
            [
                jnp.sum(
                    pltpu.roll(
                        kept[at : at + per_row], 0, 1, stride=group, stride_axis=0
                    ),
                    axis=0,
                    keepdims=True,
                )
                for at in range(0, n, per_row)
            ],
            axis=1,
        )

    vector = spread_out(got)
    diagonal = spread_out(pltpu.roll(got, 128 - group, 1))
    scale_total = jnp.sum(diagonal, axis=1, keepdims=True) + (members - 1.0)
    inverse_scale = 1.0 / scale_total

    corner = sr[:, : group // 2].reshape(half, 128)
    both = sr[:, group // 2 : group].reshape(half, 128)
    flipped = both.T
    lower = jnp.where(row > column, both, flipped)
    upper = jnp.where(row < column, both, flipped)
    full = jnp.concatenate(
        [
            jnp.concatenate([lower, corner], axis=1),
            jnp.concatenate([corner.T, upper], axis=1),
        ],
        axis=0,
    )
    full_row = lax.broadcasted_iota(jnp.int32, (members, members), 0)
    full_column = lax.broadcasted_iota(jnp.int32, (members, members), 1)
    on_diagonal = full_row == full_column
    full = jnp.where(on_diagonal, diagonal + (members - 1.0), full) * inverse_scale

    def middle_of(product):
        return jnp.where(on_diagonal, 1.5, 0.0) - 0.5 * product

    def store(where, values):
        hi, lo = split(values)
        hi_ref[where] = hi
        lo_ref[where] = lo

    top, bottom = pl.ds(0, members), pl.ds(members, members)

    def product():
        return dot3(
            (hi_ref[bottom], lo_ref[bottom]), (hi_ref[top], lo_ref[top])
        )

    first = middle_of(full)
    store(top, dot3(split(full), split(first)))
    store(bottom, first)

    def iterate(step, carry):
        middle = split(middle_of(product()))
        store(pl.ds(0, 2 * members), dot3((hi_ref[...], lo_ref[...]), middle))
        return carry

    lax.fori_loop(1, ITERS - 1, iterate, 0)
    middle = split(middle_of(product()))
    inverse_root = dot3((hi_ref[bottom], lo_ref[bottom]), middle)
    root_parts = split(inverse_root)
    inner = dot3(split(jnp.broadcast_to(vector, (8, members))), root_parts)
    shift = dot3(split(inner), root_parts)[0:1] * inverse_scale
    spread = jnp.sqrt((members - 1.0) * inverse_scale)
    combined = split(inverse_root * spread + shift)

    own_background.wait()
    take(xin.at[all_but_one], recv_sem.at[3])
    values = split(xin[...].reshape(members, xin.shape[2]))
    mean = mean_ref[...]
    og[...] = (dot3(combined, values) + mean).reshape(og.shape)
    result_copy = exchange(
        4, lambda to: og.at[to], lambda slot: out_ref.at[:, slot, :]
    )
    each(lambda j: result_copy(j).start())
    own_result = pltpu.make_async_copy(
        og.at[me], out_ref.at[:, me, :], local_sem.at[2]
    )
    own_result.start()
    own_result.wait()
    for copy in extra_near:
        copy.wait_send()
    pair_copy.wait_send()

    take(cs.at[0], near_send.at[2])
    take(cs.at[2], near_send.at[3])
    take(xa.at[all_but_one], send_sem.at[0])
    take(cf.at[all_but_one], send_sem.at[1])
    take(sp.at[all_but_one, used], send_sem.at[2])
    take(xin.at[all_but_one], send_sem.at[3])
    take(og.at[all_but_one], send_sem.at[4])
    take(og.at[all_but_one], recv_sem.at[4])


def on_device(n, regions, perturb, mean_state, obs_pert, depart, inv_var, lists, counts):
    group, tiles, cells = perturb.shape
    blocks = depart.shape[0]
    members = n * group
    f32 = jnp.float32
    hbm = pl.BlockSpec(memory_space=pltpu.HBM)
    return pl.pallas_call(
        functools.partial(kernel, n, regions),
        out_shape=jax.ShapeDtypeStruct((group, tiles, cells), f32),
        in_specs=[hbm] * 7,
        out_specs=pl.BlockSpec(memory_space=pl.ANY),
        scratch_shapes=[
            pltpu.SMEM(counts.shape, jnp.int32),
            pltpu.VMEM(lists.shape, jnp.int32),
            pltpu.VMEM(obs_pert.shape, f32),
            pltpu.VMEM(depart.shape, f32),
            pltpu.VMEM(inv_var.shape, f32),
            pltpu.VMEM((1, cells), f32),
            pltpu.VMEM((n, group, 128), f32),
            pltpu.VMEM((2, n, group // 2, 128), f32),
            pltpu.VMEM((n, group // 2, 128), f32),
            pltpu.VMEM((n, group // 2, 128), f32),
            pltpu.VMEM((3, blocks, 2, group // 2, 128), f32),
            pltpu.VMEM((3, blocks, 128), f32),
            pltpu.VMEM((n, group + 8, 128), f32),
            pltpu.VMEM((n, group + 8, 128), f32),
            pltpu.VMEM((n, group, cells), f32),
            pltpu.VMEM((n, group, cells), f32),
            pltpu.VMEM((2 * members, members), jnp.bfloat16),
            pltpu.VMEM((2 * members, members), jnp.bfloat16),
            pltpu.SemaphoreType.DMA((5,)),
            pltpu.SemaphoreType.DMA((5,)),
            pltpu.SemaphoreType.DMA((n // 2,)),
            pltpu.SemaphoreType.DMA((4,)),
            pltpu.SemaphoreType.DMA((4,)),
            pltpu.SemaphoreType.DMA,
            pltpu.SemaphoreType.DMA,
            pltpu.SemaphoreType.DMA((9,)),
            pltpu.SemaphoreType.REGULAR,
            pltpu.SemaphoreType.REGULAR,
        ],
        compiler_params=pltpu.CompilerParams(
            collective_id=0, has_side_effects=True, vmem_limit_bytes=32 * 2**20
        ),
        name="analysis",
    )(
        *[
            pltpu.with_memory_space_constraint(value, pltpu.HBM)
            for value in (counts, lists, obs_pert, depart, inv_var, mean_state, perturb)
        ]
    )


def solution(mesh):
    placed = (
        P("mem", "reg", None),
        P("reg", None),
        P("mem", "reg", None),
        P("reg", None),
        P("reg", None),
        P("reg", None),
        P("reg"),
    )
    return jax.shard_map(
        functools.partial(on_device, mesh.shape["mem"], mesh.shape["reg"]),
        mesh=mesh,
        in_specs=placed,
        out_specs=P("mem", "reg", None),
        check_vma=False,
    )
```

```python
import functools

import jax
import jax.numpy as jnp
from jax import lax
from jax.experimental import pallas as pl
from jax.experimental.pallas import tpu as pltpu
from jax.sharding import PartitionSpec as P

ITERS = 6
PLAN = ((), (4,), (2, 6), (1, 7, 0), (3, 5))
FIRST = ((), (3, 5), (4, 1, 7, 0), (), (2, 6))
LAST = ((), (4,), (), (1, 7, 0, 2, 6), (3, 5))

MESH = pl.DeviceIdType.MESH
NT = (((1,), (1,)), ((), ()))
NN = (((1,), (0,)), ((), ()))


def split(a):
    hi = a.astype(jnp.bfloat16)
    return hi, (a - hi.astype(jnp.float32)).astype(jnp.bfloat16)


def dot3(a, b, dims=NN):
    def one(x, y):
        return lax.dot_general(x, y, dims, preferred_element_type=jnp.float32)

    return one(a[0], b[0]) + (one(a[0], b[1]) + one(a[1], b[0]))


def kernel(
    n,
    regions,
    counts_in,
    lists_in,
    obs_in,
    depart_in,
    inv_in,
    mean_in,
    perturb_ref,
    out_ref,
    counts_ref,
    lists_ref,
    obs_ref,
    depart_ref,
    inv_ref,
    mean_ref,
    xa,
    cp,
    pr,
    cf,
    cs,
    ex,
    sp,
    sr,
    xin,
    og,
    hi_ref,
    lo_ref,
    send_sem,
    recv_sem,
    chip_sem,
    near_send,
    near_recv,
    pair_send,
    pair_recv,
    local_sem,
    group_in,
    near_in,
):
    me = lax.axis_index("mem")
    region = lax.axis_index("reg")
    right = lax.rem(region + 1, regions)
    left = lax.rem(region + regions - 1, regions)
    blocks = depart_in.shape[0]
    group = obs_in.shape[0]
    members = n * group
    half = members // 2
    others = n - 1
    chips = n // 2
    chip = me // 2
    core = lax.rem(me, 2)

    def partner(j):
        return 2 * lax.rem(chip + j // 2, chips) + lax.rem(core + lax.rem(j, 2), 2)

    def exchange(phase, source, target, arrival=None):
        def copy(j):
            to = partner(j)
            landed = recv_sem.at[phase] if arrival is None else arrival(j)
            return pltpu.make_async_remote_copy(
                src_ref=source(to),
                dst_ref=target(me),
                send_sem=send_sem.at[phase],
                recv_sem=landed,
                device_id=(to, region),
                device_id_type=MESH,
            )

        return copy

    def take(ref, sem):
        pltpu.make_async_copy(ref, ref, sem).wait()

    all_but_one = pl.ds(0, others)

    chip_order = [
        chips // 2 + (i + 1) // 2 * (1 - 2 * (i % 2)) for i in range(chips)
    ]

    def each(action):
        for ahead in chip_order:
            for flip in (1, 0):
                if ahead or flip:
                    action(2 * ahead + flip)

    def near(slot, source, low, high):
        first = pltpu.make_async_remote_copy(
            src_ref=source,
            dst_ref=low,
            send_sem=near_send.at[slot],
            recv_sem=near_recv.at[slot],
            device_id=(me, right),
            device_id_type=MESH,
        )
        second = pltpu.make_async_remote_copy(
            src_ref=source,
            dst_ref=high,
            send_sem=near_send.at[slot + 1],
            recv_sem=near_recv.at[slot + 1],
            device_id=(me, left),
            device_id_type=MESH,
        )
        return first, second

    lead = 0
    leads = me == lead
    follows = me != lead
    barrier = pltpu.get_barrier_semaphore()

    def greet(j):
        to = partner(j)

        @pl.when(to != lead)
        def _():
            pl.semaphore_signal(
                barrier, inc=1, device_id=(to, region), device_id_type=MESH
            )

    each(greet)

    loads = [
        pltpu.make_async_copy(source, target, local_sem.at[3 + at])
        for at, (source, target) in enumerate(
            (
                (counts_in, counts_ref),
                (lists_in, lists_ref),
                (obs_in, obs_ref),
                (depart_in, depart_ref),
                (inv_in, inv_ref),
                (mean_in.at[pl.ds(me, 1)], mean_ref),
            )
        )
    ]
    for load in loads:
        load.start()
    own_background = pltpu.make_async_copy(
        perturb_ref.at[:, me, :], xin.at[me], local_sem.at[1]
    )
    own_background.start()
    background = exchange(
        3, lambda to: perturb_ref.at[:, to, :], lambda slot: xin.at[slot]
    )

    @pl.when(follows)
    def _():
        pl.semaphore_wait(barrier, others)

    @pl.when(me == lead + 1)
    def _():
        pl.semaphore_signal(
            group_in, inc=1, device_id=(lead, region), device_id_type=MESH
        )
        for side in (left, right):
            pl.semaphore_signal(
                barrier, inc=1, device_id=(lead, side), device_id_type=MESH
            )

    @pl.when(leads)
    def _():
        pl.semaphore_wait(group_in, 1)

    def piece(to):
        return obs_in.at[
            :, to // 2, pl.ds(pl.multiple_of(lax.rem(to, 2) * 128, 128), 128)
        ]

    obs_copy = exchange(0, piece, lambda slot: xa.at[slot])

    def send_background(point):
        begins, ends = region == 0, region == regions - 1
        for here, plan in (
            (begins, FIRST),
            (ends, LAST),
            (jnp.logical_not(begins | ends), PLAN),
        ):
            if not plan[point]:
                continue

            @pl.when(here)
            def _(plan=plan):
                for ahead in plan[point]:
                    for flip in (0, 1):
                        if ahead or flip:
                            background(2 * ahead + flip).start()

    send_background(0)
    each(lambda j: obs_copy(j).start())
    own_obs = pltpu.make_async_copy(piece(me), xa.at[me], local_sem.at[0])
    own_obs.start()
    send_background(1)
    for load in loads:
        load.wait()

    tile_row = lax.broadcasted_iota(jnp.int32, (n, 128), 0)
    lane = lax.broadcasted_iota(jnp.int32, (n, 128), 1)
    live = jnp.zeros((n, 128), jnp.int32)
    for t in range(n):
        live = jnp.where(tile_row == t, counts_ref[t], live)
    total = blocks * regions
    local = lax.rem(lists_ref[...] - region * blocks + (blocks + total), total)
    chosen = jnp.zeros((n, 128), jnp.float32)
    for j in range(lists_ref.shape[1]):
        hit = (lane == local[:, j : j + 1]) & (live > j)
        chosen = jnp.where(hit, 1.0, chosen)
    chosen = chosen[:, : 3 * blocks].astype(jnp.bfloat16)

    weights = inv_ref[...]
    weighted_departures = weights * depart_ref[...]
    extra_lane = lax.broadcasted_iota(jnp.int32, (blocks, 128), 1)
    extras = jnp.zeros((blocks, 128), jnp.float32)
    for i in range(group):
        one = obs_ref[i]
        vector = jnp.sum(one * weighted_departures, axis=1, keepdims=True)
        diagonal = jnp.sum(one * one * weights, axis=1, keepdims=True)
        extras = jnp.where(extra_lane == i, vector, extras)
        extras = jnp.where(extra_lane == group + i, diagonal, extras)
    ex[1] = extras

    def combine(values):
        top = values.astype(jnp.bfloat16)
        rest = values - top.astype(jnp.float32)
        middle = rest.astype(jnp.bfloat16)
        last = (rest - middle.astype(jnp.float32)).astype(jnp.bfloat16)
        parts = [
            jnp.dot(chosen, part, preferred_element_type=jnp.float32)
            for part in (top, middle, last)
        ]
        return parts[0] + (parts[1] + parts[2])

    own_obs.wait()
    take(xa.at[all_but_one], recv_sem.at[0])
    x = xa[...].reshape(members, 128)
    block_row = lax.broadcasted_iota(jnp.int32, weights.shape, 0)
    w = jnp.sum(
        jnp.where(block_row == me // 2, weights, 0.0), axis=0, keepdims=True
    )
    w = jnp.where(lax.rem(me, 2) == 0, w[:, :128], w[:, 128:])
    square = dot3(split(x * w), split(x), NT)
    row = lax.broadcasted_iota(jnp.int32, (half, half), 0)
    column = lax.broadcasted_iota(jnp.int32, (half, half), 1)
    cp[0] = square[:half, half:].reshape(n, group // 2, 128)
    cp[1] = jnp.where(
        row >= column, square[:half, :half], square[half:, half:]
    ).reshape(n, group // 2, 128)
    pair_copy = pltpu.make_async_remote_copy(
        src_ref=cp.at[1 - core],
        dst_ref=pr,
        send_sem=pair_send,
        recv_sem=pair_recv,
        device_id=(2 * chip + 1 - core, region),
        device_id_type=MESH,
    )
    pair_copy.start()
    pair_copy.wait_recv()
    cf[...] = cp[core] + pr[...]
    square_copy = exchange(
        1,
        lambda to: cf.at[to],
        lambda slot: cs.at[1, slot // 2, lax.rem(slot, 2)],
        lambda j: chip_sem.at[j // 2],
    )
    each(lambda j: square_copy(j).start())
    send_background(2)
    cs[1, chip, core] = cf[me]

    def pass_word(j):
        pl.semaphore_signal(
            near_in, inc=1, device_id=(partner(j), region), device_id_type=MESH
        )

    @pl.when(leads)
    def _():
        pl.semaphore_wait(barrier, 2)
        each(pass_word)

    @pl.when(follows)
    def _():
        pl.semaphore_wait(near_in, 1)

    extra_near = near(0, ex.at[1], ex.at[0], ex.at[2])
    for copy in extra_near:
        copy.start()

    for ahead in chip_order:
        take(cs.at[1, 0] if ahead else cs.at[1, 0, 0], chip_sem.at[ahead])
        b = lax.rem(chip - ahead + chips, chips)
        for copy in near(2, cs.at[1, b], cs.at[0, b], cs.at[2, b]):
            copy.start()
    send_background(3)

    take(cs.at[0], near_recv.at[2])
    take(cs.at[2], near_recv.at[3])
    for copy in extra_near:
        copy.wait_recv()
    sp[:, group, :] = combine(ex[...].reshape(3 * blocks, 128))
    near_squares = jnp.concatenate(
        [
            cs[:, :, i // 8, i % 8, :].reshape(3 * blocks, 128)
            for i in range(group)
        ],
        axis=1,
    )
    tile_squares = combine(near_squares)
    for i in range(group):
        sp[:, i, :] = tile_squares[:, i * 128 : (i + 1) * 128]
    used = pl.ds(0, group + 1)
    tile_copy = exchange(
        2, lambda to: sp.at[to, used], lambda slot: sr.at[slot, used]
    )
    each(lambda j: tile_copy(j).start())
    sr[pl.ds(me, 1)] = sp[pl.ds(me, 1)]
    send_background(4)

    take(sr.at[all_but_one, used], recv_sem.at[2])
    got = sr[:, group, :]
    got_lane = lax.broadcasted_iota(jnp.int32, got.shape, 1)

    def spread_out(values):
        kept = jnp.where(got_lane < group, values, 0.0)
        per_row = 128 // group
        return jnp.concatenate(
            [
                jnp.sum(
                    pltpu.roll(
                        kept[at : at + per_row], 0, 1, stride=group, stride_axis=0
                    ),
                    axis=0,
                    keepdims=True,
                )
                for at in range(0, n, per_row)
            ],
            axis=1,
        )

    vector = spread_out(got)
    diagonal = spread_out(pltpu.roll(got, 128 - group, 1))
    scale_total = jnp.sum(diagonal, axis=1, keepdims=True) + (members - 1.0)
    inverse_scale = 1.0 / scale_total

    corner = sr[:, : group // 2].reshape(half, 128)
    both = sr[:, group // 2 : group].reshape(half, 128)
    flipped = both.T
    lower = jnp.where(row > column, both, flipped)
    upper = jnp.where(row < column, both, flipped)
    full = jnp.concatenate(
        [
            jnp.concatenate([lower, corner], axis=1),
            jnp.concatenate([corner.T, upper], axis=1),
        ],
        axis=0,
    )
    full_row = lax.broadcasted_iota(jnp.int32, (members, members), 0)
    full_column = lax.broadcasted_iota(jnp.int32, (members, members), 1)
    on_diagonal = full_row == full_column
    full = jnp.where(on_diagonal, diagonal + (members - 1.0), full) * inverse_scale

    def middle_of(product):
        return jnp.where(on_diagonal, 1.5, 0.0) - 0.5 * product

    def store(where, values):
        hi, lo = split(values)
        hi_ref[where] = hi
        lo_ref[where] = lo

    top, bottom = pl.ds(0, members), pl.ds(members, members)

    def product():
        return dot3(
            (hi_ref[bottom], lo_ref[bottom]), (hi_ref[top], lo_ref[top])
        )

    first = middle_of(full)
    store(top, dot3(split(full), split(first)))
    store(bottom, first)

    def iterate(step, carry):
        middle = split(middle_of(product()))
        for half_of in (top, bottom):
            store(half_of, dot3((hi_ref[half_of], lo_ref[half_of]), middle))
        return carry

    lax.fori_loop(1, ITERS - 1, iterate, 0)
    middle = split(middle_of(product()))
    inverse_root = dot3((hi_ref[bottom], lo_ref[bottom]), middle)
    root_parts = split(inverse_root)
    inner = dot3(split(jnp.broadcast_to(vector, (8, members))), root_parts)
    shift = dot3(split(inner), root_parts)[0:1] * inverse_scale
    spread = jnp.sqrt((members - 1.0) * inverse_scale)
    combined = split(inverse_root * spread + shift)

    own_background.wait()
    take(xin.at[all_but_one], recv_sem.at[3])
    values = split(xin[...].reshape(members, xin.shape[2]))
    mean = mean_ref[...]
    result_copy = exchange(
        4, lambda to: og.at[to], lambda slot: out_ref.at[:, slot, :]
    )
    for low in (0, n // 2):
        rows = slice(low * group, low * group + half)
        og[low : low + n // 2] = (
            dot3([part[rows] for part in combined], values) + mean
        ).reshape(n // 2, group, og.shape[2])

        def send(j):
            to = partner(j)

            @pl.when((to >= low) & (to < low + n // 2))
            def _():
                result_copy(j).start()

        each(send)
    own_result = pltpu.make_async_copy(
        og.at[me], out_ref.at[:, me, :], local_sem.at[2]
    )
    own_result.start()
    own_result.wait()
    for copy in extra_near:
        copy.wait_send()
    pair_copy.wait_send()

    take(cs.at[0], near_send.at[2])
    take(cs.at[2], near_send.at[3])
    take(xa.at[all_but_one], send_sem.at[0])
    take(cf.at[all_but_one], send_sem.at[1])
    take(sp.at[all_but_one, used], send_sem.at[2])
    take(xin.at[all_but_one], send_sem.at[3])
    take(og.at[all_but_one], send_sem.at[4])
    take(og.at[all_but_one], recv_sem.at[4])


def on_device(n, regions, perturb, mean_state, obs_pert, depart, inv_var, lists, counts):
    group, tiles, cells = perturb.shape
    blocks = depart.shape[0]
    members = n * group
    f32 = jnp.float32
    hbm = pl.BlockSpec(memory_space=pltpu.HBM)
    return pl.pallas_call(
        functools.partial(kernel, n, regions),
        out_shape=jax.ShapeDtypeStruct((group, tiles, cells), f32),
        in_specs=[hbm] * 7,
        out_specs=pl.BlockSpec(memory_space=pl.ANY),
        scratch_shapes=[
            pltpu.SMEM(counts.shape, jnp.int32),
            pltpu.VMEM(lists.shape, jnp.int32),
            pltpu.VMEM(obs_pert.shape, f32),
            pltpu.VMEM(depart.shape, f32),
            pltpu.VMEM(inv_var.shape, f32),
            pltpu.VMEM((1, cells), f32),
            pltpu.VMEM((n, group, 128), f32),
            pltpu.VMEM((2, n, group // 2, 128), f32),
            pltpu.VMEM((n, group // 2, 128), f32),
            pltpu.VMEM((n, group // 2, 128), f32),
            pltpu.VMEM((3, blocks, 2, group // 2, 128), f32),
            pltpu.VMEM((3, blocks, 128), f32),
            pltpu.VMEM((n, group + 8, 128), f32),
            pltpu.VMEM((n, group + 8, 128), f32),
            pltpu.VMEM((n, group, cells), f32),
            pltpu.VMEM((n, group, cells), f32),
            pltpu.VMEM((2 * members, members), jnp.bfloat16),
            pltpu.VMEM((2 * members, members), jnp.bfloat16),
            pltpu.SemaphoreType.DMA((5,)),
            pltpu.SemaphoreType.DMA((5,)),
            pltpu.SemaphoreType.DMA((n // 2,)),
            pltpu.SemaphoreType.DMA((4,)),
            pltpu.SemaphoreType.DMA((4,)),
            pltpu.SemaphoreType.DMA,
            pltpu.SemaphoreType.DMA,
            pltpu.SemaphoreType.DMA((9,)),
            pltpu.SemaphoreType.REGULAR,
            pltpu.SemaphoreType.REGULAR,
        ],
        compiler_params=pltpu.CompilerParams(
            collective_id=0, has_side_effects=True, vmem_limit_bytes=32 * 2**20
        ),
        name="analysis",
    )(
        *[
            pltpu.with_memory_space_constraint(value, pltpu.HBM)
            for value in (counts, lists, obs_pert, depart, inv_var, mean_state, perturb)
        ]
    )


def solution(mesh):
    placed = (
        P("mem", "reg", None),
        P("reg", None),
        P("mem", "reg", None),
        P("reg", None),
        P("reg", None),
        P("reg", None),
        P("reg"),
    )
    return jax.shard_map(
        functools.partial(on_device, mesh.shape["mem"], mesh.shape["reg"]),
        mesh=mesh,
        in_specs=placed,
        out_specs=P("mem", "reg", None),
        check_vma=False,
    )
```

```python
import functools

import jax
import jax.numpy as jnp
from jax import lax
from jax.experimental import pallas as pl
from jax.experimental.pallas import tpu as pltpu
from jax.sharding import PartitionSpec as P

ITERS = 6
PLAN = ((), (4,), (2, 6), (1, 7, 0), (3, 5))
FIRST = ((), (3, 5), (4, 1, 7, 0), (), (2, 6))
LAST = ((), (4,), (), (1, 7, 0, 2, 6), (3, 5))

MESH = pl.DeviceIdType.MESH
NT = (((1,), (1,)), ((), ()))
NN = (((1,), (0,)), ((), ()))


def split(a):
    hi = a.astype(jnp.bfloat16)
    return hi, (a - hi.astype(jnp.float32)).astype(jnp.bfloat16)


def dot3(a, b, dims=NN):
    def one(x, y):
        return lax.dot_general(x, y, dims, preferred_element_type=jnp.float32)

    return one(a[0], b[0]) + (one(a[0], b[1]) + one(a[1], b[0]))


def kernel(
    n,
    regions,
    counts_in,
    lists_in,
    obs_in,
    depart_in,
    inv_in,
    mean_in,
    perturb_ref,
    out_ref,
    counts_ref,
    lists_ref,
    obs_ref,
    depart_ref,
    inv_ref,
    mean_ref,
    xa,
    cp,
    pr,
    cf,
    cs,
    ex,
    sp,
    sr,
    xin,
    og,
    hi_ref,
    lo_ref,
    send_sem,
    recv_sem,
    chip_sem,
    near_send,
    near_recv,
    pair_send,
    pair_recv,
    local_sem,
    group_in,
    near_in,
):
    me = lax.axis_index("mem")
    region = lax.axis_index("reg")
    right = lax.rem(region + 1, regions)
    left = lax.rem(region + regions - 1, regions)
    blocks = depart_in.shape[0]
    group = obs_in.shape[0]
    members = n * group
    half = members // 2
    others = n - 1
    chips = n // 2
    chip = me // 2
    core = lax.rem(me, 2)

    def partner(j):
        return 2 * lax.rem(chip + j // 2, chips) + lax.rem(core + lax.rem(j, 2), 2)

    def exchange(phase, source, target, arrival=None):
        def copy(j):
            to = partner(j)
            landed = recv_sem.at[phase] if arrival is None else arrival(j)
            return pltpu.make_async_remote_copy(
                src_ref=source(to),
                dst_ref=target(me),
                send_sem=send_sem.at[phase],
                recv_sem=landed,
                device_id=(to, region),
                device_id_type=MESH,
            )

        return copy

    def take(ref, sem):
        pltpu.make_async_copy(ref, ref, sem).wait()

    all_but_one = pl.ds(0, others)

    chip_order = [
        chips // 2 + (i + 1) // 2 * (1 - 2 * (i % 2)) for i in range(chips)
    ]

    def each(action):
        for ahead in chip_order:
            for flip in (1, 0):
                if ahead or flip:
                    action(2 * ahead + flip)

    def near(slot, source, low, high):
        first = pltpu.make_async_remote_copy(
            src_ref=source,
            dst_ref=low,
            send_sem=near_send.at[slot],
            recv_sem=near_recv.at[slot],
            device_id=(me, right),
            device_id_type=MESH,
        )
        second = pltpu.make_async_remote_copy(
            src_ref=source,
            dst_ref=high,
            send_sem=near_send.at[slot + 1],
            recv_sem=near_recv.at[slot + 1],
            device_id=(me, left),
            device_id_type=MESH,
        )
        return first, second

    lead = 0
    leads = me == lead
    follows = me != lead
    barrier = pltpu.get_barrier_semaphore()

    def greet(j):
        to = partner(j)

        @pl.when(to != lead)
        def _():
            pl.semaphore_signal(
                barrier, inc=1, device_id=(to, region), device_id_type=MESH
            )

    each(greet)

    loads = [
        pltpu.make_async_copy(source, target, local_sem.at[3 + at])
        for at, (source, target) in enumerate(
            (
                (counts_in, counts_ref),
                (lists_in, lists_ref),
                (obs_in, obs_ref),
                (depart_in, depart_ref),
                (inv_in, inv_ref),
                (mean_in.at[pl.ds(me, 1)], mean_ref),
            )
        )
    ]
    for load in loads:
        load.start()
    own_background = pltpu.make_async_copy(
        perturb_ref.at[:, me, :], xin.at[me], local_sem.at[1]
    )
    own_background.start()
    background = exchange(
        3, lambda to: perturb_ref.at[:, to, :], lambda slot: xin.at[slot]
    )

    @pl.when(follows)
    def _():
        pl.semaphore_wait(barrier, others)

    @pl.when(me == lead + 1)
    def _():
        pl.semaphore_signal(
            group_in, inc=1, device_id=(lead, region), device_id_type=MESH
        )
        for side in (left, right):
            pl.semaphore_signal(
                barrier, inc=1, device_id=(lead, side), device_id_type=MESH
            )

    @pl.when(leads)
    def _():
        pl.semaphore_wait(group_in, 1)

    def piece(to):
        return obs_in.at[
            :, to // 2, pl.ds(pl.multiple_of(lax.rem(to, 2) * 128, 128), 128)
        ]

    obs_copy = exchange(0, piece, lambda slot: xa.at[slot])

    def send_background(point):
        begins, ends = region == 0, region == regions - 1
        for here, plan in (
            (begins, FIRST),
            (ends, LAST),
            (jnp.logical_not(begins | ends), PLAN),
        ):
            if not plan[point]:
                continue

            @pl.when(here)
            def _(plan=plan):
                for ahead in plan[point]:
                    for flip in (0, 1):
                        if ahead or flip:
                            background(2 * ahead + flip).start()

    send_background(0)
    each(lambda j: obs_copy(j).start())
    own_obs = pltpu.make_async_copy(piece(me), xa.at[me], local_sem.at[0])
    own_obs.start()
    send_background(1)
    for load in loads:
        load.wait()

    tile_row = lax.broadcasted_iota(jnp.int32, (n, 128), 0)
    lane = lax.broadcasted_iota(jnp.int32, (n, 128), 1)
    live = jnp.zeros((n, 128), jnp.int32)
    for t in range(n):
        live = jnp.where(tile_row == t, counts_ref[t], live)
    total = blocks * regions
    local = lax.rem(lists_ref[...] - region * blocks + (blocks + total), total)
    chosen = jnp.zeros((n, 128), jnp.float32)
    for j in range(lists_ref.shape[1]):
        hit = (lane == local[:, j : j + 1]) & (live > j)
        chosen = jnp.where(hit, 1.0, chosen)
    chosen = chosen[:, : 3 * blocks].astype(jnp.bfloat16)

    weights = inv_ref[...]
    weighted_departures = weights * depart_ref[...]
    extra_lane = lax.broadcasted_iota(jnp.int32, (blocks, 128), 1)
    extras = jnp.zeros((blocks, 128), jnp.float32)
    for i in range(group):
        one = obs_ref[i]
        vector = jnp.sum(one * weighted_departures, axis=1, keepdims=True)
        diagonal = jnp.sum(one * one * weights, axis=1, keepdims=True)
        extras = jnp.where(extra_lane == i, vector, extras)
        extras = jnp.where(extra_lane == group + i, diagonal, extras)
    ex[1] = extras

    def combine(values):
        top = values.astype(jnp.bfloat16)
        rest = values - top.astype(jnp.float32)
        middle = rest.astype(jnp.bfloat16)
        last = (rest - middle.astype(jnp.float32)).astype(jnp.bfloat16)
        parts = [
            jnp.dot(chosen, part, preferred_element_type=jnp.float32)
            for part in (top, middle, last)
        ]
        return parts[0] + (parts[1] + parts[2])

    own_obs.wait()
    take(xa.at[all_but_one], recv_sem.at[0])
    x = xa[...].reshape(members, 128)
    block_row = lax.broadcasted_iota(jnp.int32, weights.shape, 0)
    w = jnp.sum(
        jnp.where(block_row == me // 2, weights, 0.0), axis=0, keepdims=True
    )
    w = jnp.where(lax.rem(me, 2) == 0, w[:, :128], w[:, 128:])
    square = dot3(split(x * w), split(x), NT)
    row = lax.broadcasted_iota(jnp.int32, (half, half), 0)
    column = lax.broadcasted_iota(jnp.int32, (half, half), 1)
    cp[0] = square[:half, half:].reshape(n, group // 2, 128)
    cp[1] = jnp.where(
        row >= column, square[:half, :half], square[half:, half:]
    ).reshape(n, group // 2, 128)
    pair_copy = pltpu.make_async_remote_copy(
        src_ref=cp.at[1 - core],
        dst_ref=pr,
        send_sem=pair_send,
        recv_sem=pair_recv,
        device_id=(2 * chip + 1 - core, region),
        device_id_type=MESH,
    )
    pair_copy.start()
    pair_copy.wait_recv()
    cf[...] = cp[core] + pr[...]
    square_copy = exchange(
        1,
        lambda to: cf.at[to],
        lambda slot: cs.at[1, slot // 2, lax.rem(slot, 2)],
        lambda j: chip_sem.at[j // 2],
    )
    each(lambda j: square_copy(j).start())
    send_background(2)
    cs[1, chip, core] = cf[me]

    def pass_word(j):
        pl.semaphore_signal(
            near_in, inc=1, device_id=(partner(j), region), device_id_type=MESH
        )

    @pl.when(leads)
    def _():
        pl.semaphore_wait(barrier, 2)
        each(pass_word)

    @pl.when(follows)
    def _():
        pl.semaphore_wait(near_in, 1)

    extra_near = near(0, ex.at[1], ex.at[0], ex.at[2])
    for copy in extra_near:
        copy.start()

    for ahead in reversed(chip_order):
        take(cs.at[1, 0] if ahead else cs.at[1, 0, 0], chip_sem.at[ahead])
        b = lax.rem(chip - ahead + chips, chips)
        for copy in near(2, cs.at[1, b], cs.at[0, b], cs.at[2, b]):
            copy.start()
    send_background(3)

    take(cs.at[0], near_recv.at[2])
    take(cs.at[2], near_recv.at[3])
    for copy in extra_near:
        copy.wait_recv()
    sp[:, group, :] = combine(ex[...].reshape(3 * blocks, 128))
    near_squares = jnp.concatenate(
        [
            cs[:, :, i // 8, i % 8, :].reshape(3 * blocks, 128)
            for i in range(group)
        ],
        axis=1,
    )
    tile_squares = combine(near_squares)
    for i in range(group):
        sp[:, i, :] = tile_squares[:, i * 128 : (i + 1) * 128]
    used = pl.ds(0, group + 1)
    tile_copy = exchange(
        2, lambda to: sp.at[to, used], lambda slot: sr.at[slot, used]
    )
    each(lambda j: tile_copy(j).start())
    sr[pl.ds(me, 1)] = sp[pl.ds(me, 1)]
    send_background(4)

    take(sr.at[all_but_one, used], recv_sem.at[2])
    got = sr[:, group, :]
    got_lane = lax.broadcasted_iota(jnp.int32, got.shape, 1)

    def spread_out(values):
        kept = jnp.where(got_lane < group, values, 0.0)
        per_row = 128 // group
        return jnp.concatenate(
            [
                jnp.sum(
                    pltpu.roll(
                        kept[at : at + per_row], 0, 1, stride=group, stride_axis=0
                    ),
                    axis=0,
                    keepdims=True,
                )
                for at in range(0, n, per_row)
            ],
            axis=1,
        )

    vector = spread_out(got)
    diagonal = spread_out(pltpu.roll(got, 128 - group, 1))
    scale_total = jnp.sum(diagonal, axis=1, keepdims=True) + (members - 1.0)
    inverse_scale = 1.0 / scale_total

    corner = sr[:, : group // 2].reshape(half, 128)
    both = sr[:, group // 2 : group].reshape(half, 128)
    flipped = both.T
    lower = jnp.where(row > column, both, flipped)
    upper = jnp.where(row < column, both, flipped)
    full = jnp.concatenate(
        [
            jnp.concatenate([lower, corner], axis=1),
            jnp.concatenate([corner.T, upper], axis=1),
        ],
        axis=0,
    )
    full_row = lax.broadcasted_iota(jnp.int32, (members, members), 0)
    full_column = lax.broadcasted_iota(jnp.int32, (members, members), 1)
    on_diagonal = full_row == full_column
    full = jnp.where(on_diagonal, diagonal + (members - 1.0), full) * inverse_scale

    def middle_of(product):
        return jnp.where(on_diagonal, 1.5, 0.0) - 0.5 * product

    def store(where, values):
        hi, lo = split(values)
        hi_ref[where] = hi
        lo_ref[where] = lo

    top, bottom = pl.ds(0, members), pl.ds(members, members)

    def product():
        return dot3(
            (hi_ref[bottom], lo_ref[bottom]), (hi_ref[top], lo_ref[top])
        )

    first = middle_of(full)
    store(top, dot3(split(full), split(first)))
    store(bottom, first)

    def iterate(step, carry):
        middle = split(middle_of(product()))
        for half_of in (top, bottom):
            store(half_of, dot3((hi_ref[half_of], lo_ref[half_of]), middle))
        return carry

    lax.fori_loop(1, ITERS - 1, iterate, 0)
    middle = split(middle_of(product()))
    inverse_root = dot3((hi_ref[bottom], lo_ref[bottom]), middle)
    root_parts = split(inverse_root)
    inner = dot3(split(jnp.broadcast_to(vector, (8, members))), root_parts)
    shift = dot3(split(inner), root_parts)[0:1] * inverse_scale
    spread = jnp.sqrt((members - 1.0) * inverse_scale)
    combined = split(inverse_root * spread + shift)

    own_background.wait()
    take(xin.at[all_but_one], recv_sem.at[3])
    values = split(xin[...].reshape(members, xin.shape[2]))
    mean = mean_ref[...]
    result_copy = exchange(
        4, lambda to: og.at[to], lambda slot: out_ref.at[:, slot, :]
    )
    for low in (0, n // 2):
        rows = slice(low * group, low * group + half)
        og[low : low + n // 2] = (
            dot3([part[rows] for part in combined], values) + mean
        ).reshape(n // 2, group, og.shape[2])

        def send(j):
            to = partner(j)

            @pl.when((to >= low) & (to < low + n // 2))
            def _():
                result_copy(j).start()

        each(send)
    own_result = pltpu.make_async_copy(
        og.at[me], out_ref.at[:, me, :], local_sem.at[2]
    )
    own_result.start()
    own_result.wait()
    for copy in extra_near:
        copy.wait_send()
    pair_copy.wait_send()

    take(cs.at[0], near_send.at[2])
    take(cs.at[2], near_send.at[3])
    take(xa.at[all_but_one], send_sem.at[0])
    take(cf.at[all_but_one], send_sem.at[1])
    take(sp.at[all_but_one, used], send_sem.at[2])
    take(xin.at[all_but_one], send_sem.at[3])
    take(og.at[all_but_one], send_sem.at[4])
    take(og.at[all_but_one], recv_sem.at[4])


def on_device(n, regions, perturb, mean_state, obs_pert, depart, inv_var, lists, counts):
    group, tiles, cells = perturb.shape
    blocks = depart.shape[0]
    members = n * group
    f32 = jnp.float32
    hbm = pl.BlockSpec(memory_space=pltpu.HBM)
    return pl.pallas_call(
        functools.partial(kernel, n, regions),
        out_shape=jax.ShapeDtypeStruct((group, tiles, cells), f32),
        in_specs=[hbm] * 7,
        out_specs=pl.BlockSpec(memory_space=pl.ANY),
        scratch_shapes=[
            pltpu.SMEM(counts.shape, jnp.int32),
            pltpu.VMEM(lists.shape, jnp.int32),
            pltpu.VMEM(obs_pert.shape, f32),
            pltpu.VMEM(depart.shape, f32),
            pltpu.VMEM(inv_var.shape, f32),
            pltpu.VMEM((1, cells), f32),
            pltpu.VMEM((n, group, 128), f32),
            pltpu.VMEM((2, n, group // 2, 128), f32),
            pltpu.VMEM((n, group // 2, 128), f32),
            pltpu.VMEM((n, group // 2, 128), f32),
            pltpu.VMEM((3, blocks, 2, group // 2, 128), f32),
            pltpu.VMEM((3, blocks, 128), f32),
            pltpu.VMEM((n, group + 8, 128), f32),
            pltpu.VMEM((n, group + 8, 128), f32),
            pltpu.VMEM((n, group, cells), f32),
            pltpu.VMEM((n, group, cells), f32),
            pltpu.VMEM((2 * members, members), jnp.bfloat16),
            pltpu.VMEM((2 * members, members), jnp.bfloat16),
            pltpu.SemaphoreType.DMA((5,)),
            pltpu.SemaphoreType.DMA((5,)),
            pltpu.SemaphoreType.DMA((n // 2,)),
            pltpu.SemaphoreType.DMA((4,)),
            pltpu.SemaphoreType.DMA((4,)),
            pltpu.SemaphoreType.DMA,
            pltpu.SemaphoreType.DMA,
            pltpu.SemaphoreType.DMA((9,)),
            pltpu.SemaphoreType.REGULAR,
            pltpu.SemaphoreType.REGULAR,
        ],
        compiler_params=pltpu.CompilerParams(
            collective_id=0, has_side_effects=True, vmem_limit_bytes=32 * 2**20
        ),
        name="analysis",
    )(
        *[
            pltpu.with_memory_space_constraint(value, pltpu.HBM)
            for value in (counts, lists, obs_pert, depart, inv_var, mean_state, perturb)
        ]
    )


def solution(mesh):
    placed = (
        P("mem", "reg", None),
        P("reg", None),
        P("mem", "reg", None),
        P("reg", None),
        P("reg", None),
        P("reg", None),
        P("reg"),
    )
    return jax.shard_map(
        functools.partial(on_device, mesh.shape["mem"], mesh.shape["reg"]),
        mesh=mesh,
        in_specs=placed,
        out_specs=P("mem", "reg", None),
        check_vma=False,
    )
```

```python
import functools

import jax
import jax.numpy as jnp
from jax import lax
from jax.experimental import pallas as pl
from jax.experimental.pallas import tpu as pltpu
from jax.sharding import PartitionSpec as P

ITERS = 6
PLAN = ((), (4,), (2, 6), (1, 7, 0), (3, 5))
FIRST = ((), (3, 5), (4, 2, 6), (), (1, 7, 0))
LAST = ((), (4,), (), (1, 7, 0, 2, 6), (3, 5))

MESH = pl.DeviceIdType.MESH
NT = (((1,), (1,)), ((), ()))
NN = (((1,), (0,)), ((), ()))


def split(a):
    hi = a.astype(jnp.bfloat16)
    return hi, (a - hi.astype(jnp.float32)).astype(jnp.bfloat16)


def dot3(a, b, dims=NN):
    def one(x, y):
        return lax.dot_general(x, y, dims, preferred_element_type=jnp.float32)

    return one(a[0], b[0]) + (one(a[0], b[1]) + one(a[1], b[0]))


def kernel(
    n,
    regions,
    counts_in,
    lists_in,
    obs_in,
    depart_in,
    inv_in,
    mean_in,
    perturb_ref,
    out_ref,
    counts_ref,
    lists_ref,
    obs_ref,
    depart_ref,
    inv_ref,
    mean_ref,
    xa,
    cp,
    pr,
    cf,
    cs,
    ex,
    sp,
    sr,
    xin,
    og,
    hi_ref,
    lo_ref,
    send_sem,
    recv_sem,
    chip_sem,
    near_send,
    near_recv,
    pair_send,
    pair_recv,
    local_sem,
    group_in,
    near_in,
):
    me = lax.axis_index("mem")
    region = lax.axis_index("reg")
    right = lax.rem(region + 1, regions)
    left = lax.rem(region + regions - 1, regions)
    blocks = depart_in.shape[0]
    group = obs_in.shape[0]
    members = n * group
    half = members // 2
    others = n - 1
    chips = n // 2
    chip = me // 2
    core = lax.rem(me, 2)

    def partner(j):
        return 2 * lax.rem(chip + j // 2, chips) + lax.rem(core + lax.rem(j, 2), 2)

    def exchange(phase, source, target, arrival=None):
        def copy(j):
            to = partner(j)
            landed = recv_sem.at[phase] if arrival is None else arrival(j)
            return pltpu.make_async_remote_copy(
                src_ref=source(to),
                dst_ref=target(me),
                send_sem=send_sem.at[phase],
                recv_sem=landed,
                device_id=(to, region),
                device_id_type=MESH,
            )

        return copy

    def take(ref, sem):
        pltpu.make_async_copy(ref, ref, sem).wait()

    all_but_one = pl.ds(0, others)

    chip_order = [
        chips // 2 + (i + 1) // 2 * (1 - 2 * (i % 2)) for i in range(chips)
    ]

    def each(action):
        for ahead in chip_order:
            for flip in (1, 0):
                if ahead or flip:
                    action(2 * ahead + flip)

    def near(slot, source, low, high):
        first = pltpu.make_async_remote_copy(
            src_ref=source,
            dst_ref=low,
            send_sem=near_send.at[slot],
            recv_sem=near_recv.at[slot],
            device_id=(me, right),
            device_id_type=MESH,
        )
        second = pltpu.make_async_remote_copy(
            src_ref=source,
            dst_ref=high,
            send_sem=near_send.at[slot + 1],
            recv_sem=near_recv.at[slot + 1],
            device_id=(me, left),
            device_id_type=MESH,
        )
        return first, second

    lead = 0
    leads = me == lead
    follows = me != lead
    barrier = pltpu.get_barrier_semaphore()

    def greet(j):
        to = partner(j)

        @pl.when(to != lead)
        def _():
            pl.semaphore_signal(
                barrier, inc=1, device_id=(to, region), device_id_type=MESH
            )

    each(greet)

    loads = [
        pltpu.make_async_copy(source, target, local_sem.at[3 + at])
        for at, (source, target) in enumerate(
            (
                (counts_in, counts_ref),
                (lists_in, lists_ref),
                (obs_in, obs_ref),
                (depart_in, depart_ref),
                (inv_in, inv_ref),
                (mean_in.at[pl.ds(me, 1)], mean_ref),
            )
        )
    ]
    for load in loads:
        load.start()
    own_background = pltpu.make_async_copy(
        perturb_ref.at[:, me, :], xin.at[me], local_sem.at[1]
    )
    own_background.start()
    background = exchange(
        3, lambda to: perturb_ref.at[:, to, :], lambda slot: xin.at[slot]
    )

    @pl.when(follows)
    def _():
        pl.semaphore_wait(barrier, others)

    @pl.when(me == lead + 1)
    def _():
        pl.semaphore_signal(
            group_in, inc=1, device_id=(lead, region), device_id_type=MESH
        )
        for side in (left, right):
            pl.semaphore_signal(
                barrier, inc=1, device_id=(lead, side), device_id_type=MESH
            )

    @pl.when(leads)
    def _():
        pl.semaphore_wait(group_in, 1)

    def piece(to):
        return obs_in.at[
            :, to // 2, pl.ds(pl.multiple_of(lax.rem(to, 2) * 128, 128), 128)
        ]

    obs_copy = exchange(0, piece, lambda slot: xa.at[slot])

    def send_background(point):
        begins, ends = region == 0, region == regions - 1
        for here, plan in (
            (begins, FIRST),
            (ends, LAST),
            (jnp.logical_not(begins | ends), PLAN),
        ):
            if not plan[point]:
                continue

            @pl.when(here)
            def _(plan=plan):
                for ahead in plan[point]:
                    for flip in (0, 1):
                        if ahead or flip:
                            background(2 * ahead + flip).start()

    send_background(0)
    each(lambda j: obs_copy(j).start())
    own_obs = pltpu.make_async_copy(piece(me), xa.at[me], local_sem.at[0])
    own_obs.start()
    send_background(1)
    for load in loads:
        load.wait()

    tile_row = lax.broadcasted_iota(jnp.int32, (n, 128), 0)
    lane = lax.broadcasted_iota(jnp.int32, (n, 128), 1)
    live = jnp.zeros((n, 128), jnp.int32)
    for t in range(n):
        live = jnp.where(tile_row == t, counts_ref[t], live)
    total = blocks * regions
    local = lax.rem(lists_ref[...] - region * blocks + (blocks + total), total)
    chosen = jnp.zeros((n, 128), jnp.float32)
    for j in range(lists_ref.shape[1]):
        hit = (lane == local[:, j : j + 1]) & (live > j)
        chosen = jnp.where(hit, 1.0, chosen)
    chosen = chosen[:, : 3 * blocks].astype(jnp.bfloat16)

    weights = inv_ref[...]
    weighted_departures = weights * depart_ref[...]
    extra_lane = lax.broadcasted_iota(jnp.int32, (blocks, 128), 1)
    extras = jnp.zeros((blocks, 128), jnp.float32)
    for i in range(group):
        one = obs_ref[i]
        vector = jnp.sum(one * weighted_departures, axis=1, keepdims=True)
        diagonal = jnp.sum(one * one * weights, axis=1, keepdims=True)
        extras = jnp.where(extra_lane == i, vector, extras)
        extras = jnp.where(extra_lane == group + i, diagonal, extras)
    ex[1] = extras

    def combine(values, columns):
        top = values.astype(jnp.bfloat16)
        rest = values - top.astype(jnp.float32)
        middle = rest.astype(jnp.bfloat16)
        last = (rest - middle.astype(jnp.float32)).astype(jnp.bfloat16)
        parts = [
            jnp.dot(
                chosen[:, columns], part, preferred_element_type=jnp.float32
            )
            for part in (top, middle, last)
        ]
        return parts[0] + (parts[1] + parts[2])

    own_obs.wait()
    take(xa.at[all_but_one], recv_sem.at[0])
    x = xa[...].reshape(members, 128)
    block_row = lax.broadcasted_iota(jnp.int32, weights.shape, 0)
    w = jnp.sum(
        jnp.where(block_row == me // 2, weights, 0.0), axis=0, keepdims=True
    )
    w = jnp.where(lax.rem(me, 2) == 0, w[:, :128], w[:, 128:])
    square = dot3(split(x * w), split(x), NT)
    row = lax.broadcasted_iota(jnp.int32, (half, half), 0)
    column = lax.broadcasted_iota(jnp.int32, (half, half), 1)
    cp[0] = square[:half, half:].reshape(n, group // 2, 128)
    cp[1] = jnp.where(
        row >= column, square[:half, :half], square[half:, half:]
    ).reshape(n, group // 2, 128)
    pair_copy = pltpu.make_async_remote_copy(
        src_ref=cp.at[1 - core],
        dst_ref=pr,
        send_sem=pair_send,
        recv_sem=pair_recv,
        device_id=(2 * chip + 1 - core, region),
        device_id_type=MESH,
    )
    pair_copy.start()
    pair_copy.wait_recv()
    cf[...] = cp[core] + pr[...]
    square_copy = exchange(
        1,
        lambda to: cf.at[to],
        lambda slot: cs.at[1, slot // 2, lax.rem(slot, 2)],
        lambda j: chip_sem.at[j // 2],
    )
    each(lambda j: square_copy(j).start())
    send_background(2)
    cs[1, chip, core] = cf[me]

    def pass_word(j):
        pl.semaphore_signal(
            near_in, inc=1, device_id=(partner(j), region), device_id_type=MESH
        )

    @pl.when(leads)
    def _():
        pl.semaphore_wait(barrier, 2)
        each(pass_word)

    @pl.when(follows)
    def _():
        pl.semaphore_wait(near_in, 1)

    extra_near = near(0, ex.at[1], ex.at[0], ex.at[2])
    for copy in extra_near:
        copy.start()

    for ahead in chip_order:
        take(cs.at[1, 0] if ahead else cs.at[1, 0, 0], chip_sem.at[ahead])
        b = lax.rem(chip - ahead + chips, chips)
        for copy in near(2, cs.at[1, b], cs.at[0, b], cs.at[2, b]):
            copy.start()
    send_background(3)

    def slices(low, high):
        return jnp.concatenate(
            [
                cs[low:high, :, i // 8, i % 8, :].reshape((high - low) * blocks, 128)
                for i in range(group)
            ],
            axis=1,
        )

    for copy in extra_near:
        copy.wait_recv()
    sp[:, group, :] = combine(ex[...].reshape(3 * blocks, 128), slice(0, 3 * blocks))
    take(cs.at[2], near_recv.at[3])
    tile_squares = combine(slices(1, 3), slice(blocks, 3 * blocks))
    take(cs.at[0], near_recv.at[2])
    tile_squares = tile_squares + combine(slices(0, 1), slice(0, blocks))
    for i in range(group):
        sp[:, i, :] = tile_squares[:, i * 128 : (i + 1) * 128]
    used = pl.ds(0, group + 1)
    tile_copy = exchange(
        2, lambda to: sp.at[to, used], lambda slot: sr.at[slot, used]
    )
    each(lambda j: tile_copy(j).start())
    sr[pl.ds(me, 1)] = sp[pl.ds(me, 1)]
    send_background(4)

    take(sr.at[all_but_one, used], recv_sem.at[2])
    got = sr[:, group, :]
    got_lane = lax.broadcasted_iota(jnp.int32, got.shape, 1)

    def spread_out(values):
        kept = jnp.where(got_lane < group, values, 0.0)
        per_row = 128 // group
        return jnp.concatenate(
            [
                jnp.sum(
                    pltpu.roll(
                        kept[at : at + per_row], 0, 1, stride=group, stride_axis=0
                    ),
                    axis=0,
                    keepdims=True,
                )
                for at in range(0, n, per_row)
            ],
            axis=1,
        )

    vector = spread_out(got)
    diagonal = spread_out(pltpu.roll(got, 128 - group, 1))
    scale_total = jnp.sum(diagonal, axis=1, keepdims=True) + (members - 1.0)
    inverse_scale = 1.0 / scale_total

    corner = sr[:, : group // 2].reshape(half, 128)
    both = sr[:, group // 2 : group].reshape(half, 128)
    flipped = both.T
    lower = jnp.where(row > column, both, flipped)
    upper = jnp.where(row < column, both, flipped)
    full = jnp.concatenate(
        [
            jnp.concatenate([lower, corner], axis=1),
            jnp.concatenate([corner.T, upper], axis=1),
        ],
        axis=0,
    )
    full_row = lax.broadcasted_iota(jnp.int32, (members, members), 0)
    full_column = lax.broadcasted_iota(jnp.int32, (members, members), 1)
    on_diagonal = full_row == full_column
    full = jnp.where(on_diagonal, diagonal + (members - 1.0), full) * inverse_scale

    def middle_of(product):
        return jnp.where(on_diagonal, 1.5, 0.0) - 0.5 * product

    def store(where, values):
        hi, lo = split(values)
        hi_ref[where] = hi
        lo_ref[where] = lo

    top, bottom = pl.ds(0, members), pl.ds(members, members)

    def product():
        return dot3(
            (hi_ref[bottom], lo_ref[bottom]), (hi_ref[top], lo_ref[top])
        )

    first = middle_of(full)
    store(top, dot3(split(full), split(first)))
    store(bottom, first)

    def iterate(step, carry):
        middle = split(middle_of(product()))
        for half_of in (top, bottom):
            store(half_of, dot3((hi_ref[half_of], lo_ref[half_of]), middle))
        return carry

    lax.fori_loop(1, ITERS - 1, iterate, 0)
    roots = (hi_ref[bottom], lo_ref[bottom])
    carried = dot3(split(jnp.broadcast_to(vector, (8, members))), roots)
    middle = split(middle_of(product()))
    inverse_root = dot3(roots, middle)
    inner = dot3(split(carried), middle)
    shift = dot3(split(inner), split(inverse_root))[0:1] * inverse_scale
    spread = jnp.sqrt((members - 1.0) * inverse_scale)
    combined = split(inverse_root * spread + shift)

    own_background.wait()
    take(xin.at[all_but_one], recv_sem.at[3])
    values = split(xin[...].reshape(members, xin.shape[2]))
    mean = mean_ref[...]
    result_copy = exchange(
        4, lambda to: og.at[to], lambda slot: out_ref.at[:, slot, :]
    )
    for low in (0, n // 2):
        rows = slice(low * group, low * group + half)
        og[low : low + n // 2] = (
            dot3([part[rows] for part in combined], values) + mean
        ).reshape(n // 2, group, og.shape[2])

        def send(j):
            to = partner(j)

            @pl.when((to >= low) & (to < low + n // 2))
            def _():
                result_copy(j).start()

        each(send)
    own_result = pltpu.make_async_copy(
        og.at[me], out_ref.at[:, me, :], local_sem.at[2]
    )
    own_result.start()
    own_result.wait()
    for copy in extra_near:
        copy.wait_send()
    pair_copy.wait_send()

    take(cs.at[0], near_send.at[2])
    take(cs.at[2], near_send.at[3])
    take(xa.at[all_but_one], send_sem.at[0])
    take(cf.at[all_but_one], send_sem.at[1])
    take(sp.at[all_but_one, used], send_sem.at[2])
    take(xin.at[all_but_one], send_sem.at[3])
    take(og.at[all_but_one], send_sem.at[4])
    take(og.at[all_but_one], recv_sem.at[4])


def on_device(n, regions, perturb, mean_state, obs_pert, depart, inv_var, lists, counts):
    group, tiles, cells = perturb.shape
    blocks = depart.shape[0]
    members = n * group
    f32 = jnp.float32
    hbm = pl.BlockSpec(memory_space=pltpu.HBM)
    return pl.pallas_call(
        functools.partial(kernel, n, regions),
        out_shape=jax.ShapeDtypeStruct((group, tiles, cells), f32),
        in_specs=[hbm] * 7,
        out_specs=pl.BlockSpec(memory_space=pl.ANY),
        scratch_shapes=[
            pltpu.SMEM(counts.shape, jnp.int32),
            pltpu.VMEM(lists.shape, jnp.int32),
            pltpu.VMEM(obs_pert.shape, f32),
            pltpu.VMEM(depart.shape, f32),
            pltpu.VMEM(inv_var.shape, f32),
            pltpu.VMEM((1, cells), f32),
            pltpu.VMEM((n, group, 128), f32),
            pltpu.VMEM((2, n, group // 2, 128), f32),
            pltpu.VMEM((n, group // 2, 128), f32),
            pltpu.VMEM((n, group // 2, 128), f32),
            pltpu.VMEM((3, blocks, 2, group // 2, 128), f32),
            pltpu.VMEM((3, blocks, 128), f32),
            pltpu.VMEM((n, group + 8, 128), f32),
            pltpu.VMEM((n, group + 8, 128), f32),
            pltpu.VMEM((n, group, cells), f32),
            pltpu.VMEM((n, group, cells), f32),
            pltpu.VMEM((2 * members, members), jnp.bfloat16),
            pltpu.VMEM((2 * members, members), jnp.bfloat16),
            pltpu.SemaphoreType.DMA((5,)),
            pltpu.SemaphoreType.DMA((5,)),
            pltpu.SemaphoreType.DMA((n // 2,)),
            pltpu.SemaphoreType.DMA((4,)),
            pltpu.SemaphoreType.DMA((4,)),
            pltpu.SemaphoreType.DMA,
            pltpu.SemaphoreType.DMA,
            pltpu.SemaphoreType.DMA((9,)),
            pltpu.SemaphoreType.REGULAR,
            pltpu.SemaphoreType.REGULAR,
        ],
        compiler_params=pltpu.CompilerParams(
            collective_id=0, has_side_effects=True, vmem_limit_bytes=32 * 2**20
        ),
        name="analysis",
    )(
        *[
            pltpu.with_memory_space_constraint(value, pltpu.HBM)
            for value in (counts, lists, obs_pert, depart, inv_var, mean_state, perturb)
        ]
    )


def solution(mesh):
    placed = (
        P("mem", "reg", None),
        P("reg", None),
        P("mem", "reg", None),
        P("reg", None),
        P("reg", None),
        P("reg", None),
        P("reg"),
    )
    return jax.shard_map(
        functools.partial(on_device, mesh.shape["mem"], mesh.shape["reg"]),
        mesh=mesh,
        in_specs=placed,
        out_specs=P("mem", "reg", None),
        check_vma=False,
    )
```
